32 devices in a mesh: dp: 32 (over z, y, x, core).
Axes of the slice: x: 2, y: 2, z: 4, core: 2. Of those that a mesh axis runs over, the one named last changes fastest.
Arguments:
- tokens: bfloat16 [32768, 1024], P('dp'), may hold values from -6 to 6
- cotangent: bfloat16 [32768, 1024], P('dp'), may hold values from -6 to 6
- seq_lengths: int32 [32, 4], P('dp'), may hold values from 1 to 512, 1024 in all within a row
- live_seqs: int32 [32], P('dp'), may hold values from 2 to 4
- qkv_weight: bfloat16 [1024, 3072], P('dp'), may hold values from -0.1875 to 0.1875
- qkv_bias: bfloat16 [3072], P('dp'), may hold values from -2 to 2
- out_weight: bfloat16 [1024, 1024], P('dp'), may hold values from -1 to 1
- out_bias: bfloat16 [1024], P('dp'), may hold values from -2 to 2
- up_weight: bfloat16 [1024, 4096], P('dp'), may hold values from -0.1875 to 0.1875
- up_bias: bfloat16 [4096], P('dp'), may hold values from -3 to 3
- down_weight: bfloat16 [4096, 1024], P('dp'), may hold values from -0.09375 to 0.09375
- down_bias: bfloat16 [1024], P('dp'), may hold values from -2 to 2
- attn_gain: bfloat16 [1024], P('dp'), may hold values from 0.5 to 1.5
- attn_shift: bfloat16 [1024], P('dp'), may hold values from -2 to 2
- mlp_gain: bfloat16 [1024], P('dp'), may hold values from 0.5 to 1.5
- mlp_shift: bfloat16 [1024], P('dp'), may hold values from -2 to 2
Outputs:
- mixed: bfloat16 [32768, 1024], P('dp')
- token_grad: float32 [32768, 1024], P('dp')
- qkv_weight_grad: float32 [1024, 3072], P('dp')
- qkv_bias_grad: float32 [3072], P('dp')
- out_weight_grad: float32 [1024, 1024], P('dp')
- out_bias_grad: float32 [1024], P('dp')
- up_weight_grad: float32 [1024, 4096], P('dp')
- up_bias_grad: float32 [4096], P('dp')
- down_weight_grad: float32 [4096, 1024], P('dp')
- down_bias_grad: float32 [1024], P('dp')
- attn_gain_grad: float32 [1024], P('dp')
- attn_shift_grad: float32 [1024], P('dp')
- mlp_gain_grad: float32 [1024], P('dp')
- mlp_shift_grad: float32 [1024], P('dp')
The draws below stay inside these ranges and needn't reach their ends.
Inputs may be any that keep to these rules, and one draw needn't show every extreme that they name: `seq_lengths`: each row holds the lengths of one device's 4 sequences, which fill its 1024 slots exactly; every row has one sequence of exactly 512. A device's first live_seqs sequences are live, the rest are padding whose cotangent is dropped.
All inputs are finite; a program needn't handle non-finite values.
Results may differ from the reference program's by a relative error of at most 0.0095.
Values may be sent and summed in bfloat16 or wider, within the bound.
A program may use at most 256 MiB of HBM per device.

```python
import math
import jax
import jax.numpy as jnp
import numpy as np
from jax import lax

D = 1024
HEADS = 16
HEAD = 64
FF = 4096
ROT = 16
SEQ_MAX = 512
TOK_DEV = 1024
SLOTS = 4
TOKENS = 32768
N_DP = 32


def with_ends(array, key, least, high):
    longest = array.shape.index(max(array.shape))
    spots = []
    for shift in (0, 1):
        where = [jax.random.randint(jax.random.fold_in(key, axis), (), 0, length) for axis, length in enumerate(array.shape)]
        where[longest] = (where[longest] + shift) % array.shape[longest]
        spots.append(tuple(where))
    return array.at[spots[0]].set(least).at[spots[1]].set(high)


def block_scale(key, shape, split, least, high):
    def one(position, shards_of):
        steps = jax.random.uniform(jax.random.fold_in(jax.random.fold_in(key, 6), position), (shards_of,), jnp.float32, least / len(split), high / len(split))
        return jnp.repeat(jnp.exp(steps), shape[position] // shards_of).reshape((-1,) + (1,) * (len(shape) - position - 1))

    factor_of = one(*split[0])
    for cut in split[1:]:
        factor_of = factor_of * one(*cut)
    return factor_of


def profile(count, total, limit, slope):
    portions = [(1 << 20) // math.isqrt(grade ** slope) + 1 for grade in range(2, count + 1)]
    surplus, counts = total - limit - (count - 1), [1] * (count - 1)
    while surplus > 0:
        free = [i for i in range(count - 1) if counts[i] < limit]
        mass, budget = sum([portions[i] for i in free]), surplus
        for i in free:
            extra = min(limit - counts[i], max(1, budget * portions[i] // mass), surplus)
            counts[i] = counts[i] + extra
            surplus = surplus - extra
    return np.array([limit] + counts)


def ragged(own_key, amount, total, bound, lean):
    if amount == 2:
        one = jax.random.randint(own_key, (), max(1, total - bound), min(bound, total - 1) + 1)
        return jnp.stack([one, total - one])
    tallies = jnp.asarray(profile(amount, total, bound, lean), jnp.int32)
    couples = (amount - 1) // 2
    donor, taker = tallies[1:1 + 2 * couples:2], tallies[2:2 + 2 * couples:2]
    room = jnp.minimum(donor - 1, bound - taker)
    moved = jax.random.randint(jax.random.fold_in(own_key, 1), (couples,), 0, 1 << 20) % (room + 1)
    tallies = tallies.at[1:1 + 2 * couples:2].set(donor - moved).at[2:2 + 2 * couples:2].set(taker + moved)
    return tallies[jax.random.permutation(jax.random.fold_in(own_key, 2), amount)]


def noise(key, extent, width, reach, cuts=(), kind=jnp.bfloat16):
    level = block_scale(key, extent, cuts, -0.22, 0.18) if cuts else 1.0
    array = jax.random.normal(key, extent, jnp.float32) * width * level
    return jnp.minimum(jnp.maximum(array, -reach), reach).astype(kind)


def setup_inputs(seed: int = 0) -> dict:
    splits = jax.random.split(jax.random.key(seed), 17)
    tokens = noise(splits[0], (TOKENS, D), 1.0, 6.0, ((0, 32),))
    cotangent = noise(splits[1], (TOKENS, D), 1.0, 6.0, ((0, 32),))
    seq_lengths = jax.vmap(lambda own: ragged(own, SLOTS, TOK_DEV, SEQ_MAX, 1))(jax.random.split(splits[2], N_DP)).reshape((N_DP, SLOTS)).astype(jnp.int32)
    live_seqs = with_ends(jax.random.randint(splits[3], (N_DP,), SLOTS // 2, SLOTS + 1), jax.random.fold_in(splits[3], 1), SLOTS // 2, SLOTS).astype(jnp.int32)
    qkv_weight = noise(splits[4], (D, 3 * D), D ** -0.5, 0.1875, ((0, 32),))
    qkv_bias = noise(splits[5], (3 * D,), 0.3, 2.0, ((0, 32),))
    out_weight = noise(splits[6], (D, D), (D // 32) ** -0.5, 1.0, ((0, 32),))
    out_bias = noise(splits[7], (D,), 0.3, 2.0, ((0, 32),))
    up_weight = noise(splits[8], (D, FF), D ** -0.5, 0.1875, ((0, 32),))
    up_bias = noise(splits[9], (FF,), 0.5, 3.0, ((0, 32),))
    down_weight = noise(splits[10], (FF, D), FF ** -0.5, 0.09375, ((0, 32),))
    down_bias = noise(splits[11], (D,), 0.3, 2.0, ((0, 32),))
    attn_gain = jnp.clip(1.0 + 0.1 * jax.random.normal(splits[12], (D,), jnp.float32), 0.5, 1.5).astype(jnp.bfloat16)
    attn_shift = noise(splits[13], (D,), 0.3, 2.0, ((0, 32),))
    mlp_gain = jnp.clip(1.0 + 0.1 * jax.random.normal(splits[14], (D,), jnp.float32), 0.5, 1.5).astype(jnp.bfloat16)
    mlp_shift = noise(splits[15], (D,), 0.3, 2.0, ((0, 32),))
    return {"tokens": tokens, "cotangent": cotangent, "seq_lengths": seq_lengths, "live_seqs": live_seqs, "qkv_weight": qkv_weight, "qkv_bias": qkv_bias, "out_weight": out_weight, "out_bias": out_bias, "up_weight": up_weight, "up_bias": up_bias, "down_weight": down_weight, "down_bias": down_bias, "attn_gain": attn_gain, "attn_shift": attn_shift, "mlp_gain": mlp_gain, "mlp_shift": mlp_shift}


EPS = 1e-05
MASKED = -1e+30
HIGH = lax.Precision.HIGHEST

@jax.custom_vjp
def low(v):
    return lax.optimization_barrier(v.astype(jnp.bfloat16)).astype(jnp.float32)

@jax.custom_vjp
def low_back(v):
    return v

def low_keep(v):
    return (low(v), None)

def low_pass(kept, grad):
    return (grad,)

def back_keep(v):
    return (v, None)

def back_low(kept, grad):
    return (low(grad),)
low.defvjp(low_keep, low_pass)
low_back.defvjp(back_keep, back_low)

def matmul(left, right):
    return jnp.dot(left, right, precision=HIGH, preferred_element_type=jnp.float32)

def layout(lengths, live_count, rows):
    ends = jnp.cumsum(lengths).astype(jnp.int32)
    starts = (ends - lengths).astype(jnp.int32)
    places = jnp.arange(rows, dtype=jnp.int32)
    segment = lax.optimization_barrier(jnp.sum((places[:, None] >= ends[None, :]).astype(jnp.int32), axis=1)).astype(jnp.int32)
    choose = segment[:, None] == jnp.arange(lengths.shape[0], dtype=jnp.int32)[None, :]
    offset = lax.optimization_barrier(jnp.sum(jnp.where(choose, starts[None, :], 0), axis=1)).astype(jnp.int32)
    live = (segment < live_count).astype(jnp.float32)
    return (segment, (places - offset).astype(jnp.int32), live)

def rotary(positions):
    half = ROT // 2
    freqs = 10000.0 ** (-(2.0 * jnp.arange(half, dtype=jnp.float32)) / ROT)
    angles = positions.astype(jnp.float32)[:, None, None] * freqs[None, None, :]
    return (jnp.cos(angles), jnp.sin(angles))

def rotate(values, cosine, sine):
    half = ROT // 2
    first = values[..., :half]
    second = values[..., half:ROT]
    return jnp.concatenate([first * cosine - second * sine, second * cosine + first * sine, values[..., ROT:]], axis=-1)

def layer(tokens, segment, positions, params):
    qkv_weight, qkv_bias, out_weight, out_bias, up_weight, up_bias, down_weight, down_bias, attn_gain, attn_shift, mlp_gain, mlp_shift = params
    rows = tokens.shape[0]
    average = lax.optimization_barrier(jnp.mean(tokens, axis=1, keepdims=True))
    centred = tokens - average
    variance = lax.optimization_barrier(jnp.mean(centred * centred, axis=1, keepdims=True))
    normed = centred * lax.rsqrt(variance + EPS)
    attn_in = low(normed * attn_gain + attn_shift)
    mlp_in = low(normed * mlp_gain + mlp_shift)
    joined = low_back(matmul(attn_in, qkv_weight) + qkv_bias)
    cosine, sine = rotary(positions)
    query = low(rotate(joined[:, :D].reshape(rows, HEADS, HEAD), cosine, sine))
    keys = low(rotate(joined[:, D:2 * D].reshape(rows, HEADS, HEAD), cosine, sine))
    values = low(joined[:, 2 * D:].reshape(rows, HEADS, HEAD))
    scores = low_back(jnp.einsum('qhd,khd->hqk', query, keys, precision=HIGH) * HEAD ** (-0.5))
    places = jnp.arange(rows, dtype=jnp.int32)
    allowed = (segment[:, None] == segment[None, :]) & (places[None, :] <= places[:, None])
    masked = jnp.where(allowed[None], scores, MASKED)
    largest = lax.optimization_barrier(jnp.max(masked, axis=-1, keepdims=True))
    weights = jnp.exp(masked - largest)
    probs = weights / lax.optimization_barrier(jnp.sum(weights, axis=-1, keepdims=True))
    heads_out = jnp.einsum('hqk,khd->qhd', low(probs), values, precision=HIGH).reshape(rows, D)
    attended = low_back(low(heads_out))
    hidden_pre = low_back(matmul(mlp_in, up_weight) + up_bias)
    hidden = low(jax.nn.gelu(hidden_pre, approximate=False))
    return tokens + matmul(attended, out_weight) + out_bias + matmul(hidden, down_weight) + down_bias

def reference(tokens, cotangent, seq_lengths, live_seqs, qkv_weight, qkv_bias, out_weight, out_bias, up_weight, up_bias, down_weight, down_bias, attn_gain, attn_shift, mlp_gain, mlp_shift):
    params = tuple((p.astype(jnp.float32) for p in (qkv_weight, qkv_bias, out_weight, out_bias, up_weight, up_bias, down_weight, down_bias, attn_gain, attn_shift, mlp_gain, mlp_shift)))
    segments, positions, live = jax.vmap(lambda lengths, count: layout(lengths, count, TOK_DEV))(seq_lengths, live_seqs)
    inputs = tokens.astype(jnp.float32).reshape(N_DP, TOK_DEV, D)
    checked = jax.checkpoint(layer)

    def forward(blocks, weights):

        def step(carry, item):
            return (carry, checked(item[0], item[1], item[2], weights))
        _, outputs = lax.scan(step, jnp.zeros((), jnp.float32), (blocks, segments, positions))
        return outputs
    outputs, pullback = jax.vjp(forward, inputs, params)
    upstream = cotangent.astype(jnp.float32).reshape(N_DP, TOK_DEV, D) * live[:, :, None]
    token_grad, grads = pullback(upstream)
    mixed = outputs.reshape(N_DP * TOK_DEV, D).astype(jnp.bfloat16)
    return (mixed, token_grad.reshape(N_DP * TOK_DEV, D), grads[0], grads[1], grads[2], grads[3], grads[4], grads[5], grads[6], grads[7], grads[8], grads[9], grads[10], grads[11])
```

```python
import jax
import jax.numpy as jnp
from jax import lax
from jax.experimental import pallas as pl
from jax.experimental.pallas import tpu as pltpu
from jax.sharding import PartitionSpec as P

D = 1024
HEADS = 16
HEAD = 64
FF = 4096
ROT = 16
QB = 256
PAIR = 128
REACH = 2
EPS = 1e-05
MASKED = -1e30


def layout(lengths, live_count, rows):
    ends = jnp.cumsum(lengths)
    starts = ends - lengths
    places = jnp.arange(rows, dtype=jnp.int32)
    segment = jnp.sum((places[:, None] >= ends[None, :]).astype(jnp.int32), axis=1)
    choose = segment[:, None] == jnp.arange(lengths.shape[0], dtype=jnp.int32)[None, :]
    offset = jnp.sum(jnp.where(choose, starts[None, :], 0), axis=1)
    live = (segment < live_count).astype(jnp.float32)
    return (offset, places - offset, live)


def rotary_lanes(positions):
    half = ROT // 2
    freqs = 10000.0 ** (-(2.0 * jnp.arange(half, dtype=jnp.float32)) / ROT)
    angles = positions.astype(jnp.float32)[:, None] * freqs[None, :]
    cosine, sine = jnp.cos(angles), jnp.sin(angles)
    rows = positions.shape[0]
    rest = HEAD - ROT
    turn = jnp.concatenate([cosine, cosine, jnp.ones((rows, rest), jnp.float32)], axis=1)
    cross = jnp.concatenate([-sine, sine, jnp.zeros((rows, rest), jnp.float32)], axis=1)
    return jnp.tile(turn, (1, PAIR // HEAD)), jnp.tile(cross, (1, PAIR // HEAD))


def outer_sum(left, right, kind=jnp.float32):
    return lax.dot_general(
        left, right, (((0,), (0,)), ((), ())), preferred_element_type=jnp.float32
    ).astype(kind)


def times_transposed(left, right):
    return lax.dot_general(
        left, right, (((1,), (1,)), ((), ())), preferred_element_type=jnp.float32
    )


def exchange(values):
    half = ROT // 2
    lane = lax.broadcasted_iota(jnp.int32, values.shape, 1)
    ahead = pltpu.roll(values, PAIR - half, 1)
    behind = pltpu.roll(values, half, 1)
    return jnp.where((lane & (HEAD - 1)) < half, ahead, behind)


def attention_kernel(
    q_in, k_in, v_in, grad_in, turn_ref, cross_ref, start_ref,
    out_ref, dq_ref, dk_ref, dv_ref,
    mask, q_low, k_low, v_low, dk_sum, dv_sum,
):
    rows = q_in.shape[0]
    blocks = rows // QB
    scale = HEAD ** (-0.5)

    @pl.when(pl.program_id(0) == 0)
    def _():
        for i in range(blocks):
            low = max(0, i - REACH) * QB
            width = (i + 1) * QB - low
            key = low + lax.broadcasted_iota(jnp.int32, (width, QB), 0)
            query = i * QB + lax.broadcasted_iota(jnp.int32, (width, QB), 1)
            start = start_ref[:, i * QB : (i + 1) * QB]
            mask[i, :width, :] = jnp.where((key >= start) & (key <= query), 0.0, MASKED)

    turn, cross = turn_ref[...], cross_ref[...]
    query = q_in[...]
    q_low[...] = ((query * turn + exchange(query) * cross).astype(jnp.bfloat16) * scale).astype(jnp.bfloat16)
    keys = k_in[...]
    k_low[...] = (keys * turn + exchange(keys) * cross).astype(jnp.bfloat16)
    v_low[...] = v_in[...].astype(jnp.bfloat16)
    dk_sum[...] = jnp.zeros_like(dk_sum)
    dv_sum[...] = jnp.zeros_like(dv_sum)
    k_turned = k_low[...].T
    v_turned = v_low[...].T
    for i in range(blocks):
        low = max(0, i - REACH) * QB
        high = (i + 1) * QB
        outs, grads = [], []
        for h in range(PAIR // HEAD):
            lanes = slice(h * HEAD, (h + 1) * HEAD)
            q = q_low[i * QB : high, lanes]
            do = grad_in[i * QB : high, lanes]
            k = k_low[low:high, lanes]
            v = v_low[low:high, lanes]
            scores = times_transposed(k, q) + mask[i, : high - low, :]
            largest = jnp.max(scores, axis=0, keepdims=True)
            weights = jnp.exp(scores - largest)
            inverse = 1.0 / jnp.sum(weights, axis=0, keepdims=True)
            probs = weights * inverse
            probs_low = probs.astype(jnp.bfloat16)
            outs.append(
                jnp.dot(v_turned[lanes, low:high], probs_low, preferred_element_type=jnp.float32)
            )
            dv_sum[low:high, lanes] += jnp.dot(probs_low, do, preferred_element_type=jnp.float32)
            weighted = times_transposed(v, do)
            inner = jnp.sum(probs * weighted, axis=0, keepdims=True)
            slope = (probs * (weighted - inner)).astype(jnp.bfloat16)
            grads.append(
                jnp.dot(k_turned[lanes, low:high], slope, preferred_element_type=jnp.float32)
            )
            dk_sum[low:high, lanes] += jnp.dot(slope, q, preferred_element_type=jnp.float32)
        out_ref[i * QB : high, :] = jnp.concatenate(outs, axis=0).T.astype(jnp.bfloat16)
        dq = jnp.concatenate(grads, axis=0).T * scale
        dq = dq * turn[i * QB : high, :] - exchange(dq) * cross[i * QB : high, :]
        dq_ref[i * QB : high, :] = dq.astype(jnp.bfloat16)
    dk = dk_sum[...]
    dk_ref[...] = (dk * turn - exchange(dk) * cross).astype(jnp.bfloat16)
    dv_ref[...] = dv_sum[...].astype(jnp.bfloat16)


def attention(joined, grad_low, turn, cross, start):
    rows = joined.shape[0]
    steps = D // PAIR
    blocks = rows // QB
    reach = min(REACH + 1, blocks) * QB

    def part(group):
        return pl.BlockSpec((rows, PAIR), lambda s: (0, s + group * steps))

    whole = pl.BlockSpec((rows, PAIR), lambda s: (0, 0))
    low = jax.ShapeDtypeStruct((rows, D), jnp.bfloat16)
    return pl.pallas_call(
        attention_kernel,
        grid=(steps,),
        in_specs=[
            part(0), part(1), part(2), part(0), whole, whole,
            pl.BlockSpec((1, rows), lambda s: (0, 0)),
        ],
        out_specs=[part(0)] * 4,
        out_shape=[low] * 4,
        scratch_shapes=[
            pltpu.VMEM((blocks, reach, QB), jnp.float32),
            pltpu.VMEM((rows, PAIR), jnp.bfloat16),
            pltpu.VMEM((rows, PAIR), jnp.bfloat16),
            pltpu.VMEM((rows, PAIR), jnp.bfloat16),
            pltpu.VMEM((rows, PAIR), jnp.float32),
            pltpu.VMEM((rows, PAIR), jnp.float32),
        ],
        compiler_params=pltpu.CompilerParams(vmem_limit_bytes=48 * 1024 * 1024),
        cost_estimate=pl.CostEstimate(
            flops=12 * 9 * HEADS * QB * QB * 256,
            bytes_accessed=24 * 1024 * 1024,
            transcendentals=9 * HEADS * QB * QB,
        ),
    )(joined, joined, joined, grad_low, turn, cross, start)


def gather(shard):
    return lax.all_gather(shard, "dp", axis=0, tiled=False)


def scatter(full):
    return lax.psum_scatter(full, "dp", scatter_dimension=0, tiled=True)


def make(count):
    def per_device(
        tokens, cotangent, seq_lengths, live_seqs,
        qkv_weight, qkv_bias, out_weight, out_bias, up_weight, up_bias, down_weight, down_bias,
        attn_gain, attn_shift, mlp_gain, mlp_shift,
    ):
        rows = tokens.shape[0]
        start, positions, live = layout(seq_lengths[0], live_seqs[0], rows)
        turn, cross = rotary_lanes(positions)
        small = (up_bias, mlp_gain, mlp_shift, qkv_bias, out_bias, down_bias, attn_gain, attn_shift)
        sizes = [member.shape[0] for member in small]
        packed = jnp.concatenate(small)
        packed = jnp.pad(packed, (0, FF - packed.shape[0]))[None, :]
        up_all = gather(jnp.concatenate([up_weight, packed], axis=0))
        local = up_weight.shape[0]
        up_full = up_all[:, :local].reshape(count * local, FF)
        pieces, begin = [], 0
        for size in sizes:
            piece = up_all[:, local, begin : begin + size].reshape(count * size)
            pieces.append(piece.astype(jnp.float32))
            begin += size
        hidden_bias, mlp_scale, mlp_offset, joined_bias, attn_bias, mlp_bias, attn_scale, attn_offset = pieces
        down_full = gather(down_weight).reshape(FF, D)
        qkv_full = gather(qkv_weight).reshape(D, 3 * D)
        out_full = gather(out_weight).reshape(D, D)

        inputs = tokens.astype(jnp.float32)
        average = jnp.mean(inputs, axis=1, keepdims=True)
        centred = inputs - average
        variance = jnp.mean(centred * centred, axis=1, keepdims=True)
        inverse = lax.rsqrt(variance + EPS)
        normed = centred * inverse
        attn_in = (normed * attn_scale + attn_offset).astype(jnp.bfloat16)
        mlp_in = (normed * mlp_scale + mlp_offset).astype(jnp.bfloat16)
        out_low = cotangent * live[:, None].astype(jnp.bfloat16)
        out_grad = out_low.astype(jnp.float32)

        hidden_pre = jnp.dot(mlp_in, up_full, preferred_element_type=jnp.float32) + hidden_bias
        share = 0.5 * (1.0 + lax.erf(hidden_pre * (0.5**0.5)))
        density = jnp.exp(-0.5 * hidden_pre * hidden_pre) * 0.3989422804014327
        hidden = (hidden_pre * share).astype(jnp.bfloat16)
        bend = (share + hidden_pre * density).astype(jnp.bfloat16)
        hidden, bend = lax.optimization_barrier((hidden, bend))
        down_grad = outer_sum(hidden, out_low, jnp.bfloat16)
        pre_grad = (times_transposed(out_low, down_full) * bend.astype(jnp.float32)).astype(jnp.bfloat16)
        up_grad = outer_sum(mlp_in, pre_grad, jnp.bfloat16)
        owned_down = scatter(down_grad)
        owned_up = scatter(up_grad)

        joined = jnp.dot(attn_in, qkv_full, preferred_element_type=jnp.float32) + joined_bias
        attended_grad = times_transposed(out_low, out_full).astype(jnp.bfloat16)
        attended, dq, dk, dv = attention(joined, attended_grad, turn, cross, start[None, :])
        joined_grad = jnp.concatenate([dq, dk, dv], axis=1)
        out_wgrad = outer_sum(attended, out_low, jnp.bfloat16)
        qkv_wgrad = outer_sum(attn_in, joined_grad, jnp.bfloat16)

        mlp_in_grad = times_transposed(pre_grad, up_full)
        attn_in_grad = times_transposed(joined_grad, qkv_full)
        vectors = (
            jnp.sum(joined_grad.astype(jnp.float32), axis=0),
            jnp.sum(out_grad, axis=0),
            jnp.sum(pre_grad.astype(jnp.float32), axis=0),
            jnp.sum(attn_in_grad * normed, axis=0),
            jnp.sum(attn_in_grad, axis=0),
            jnp.sum(mlp_in_grad * normed, axis=0),
            jnp.sum(mlp_in_grad, axis=0),
        )
        widths = [v.shape[0] // count for v in vectors]
        flat = jnp.concatenate([v.reshape(count, -1) for v in vectors], axis=1).astype(jnp.bfloat16)
        flat = jnp.pad(flat, ((0, 0), (0, D - flat.shape[1])))
        last = jnp.concatenate([out_wgrad.reshape(count, local, D), flat[:, None, :]], axis=1)
        owned_qkv = scatter(qkv_wgrad)
        owned_last = scatter(last)[0].astype(jnp.float32)
        owned_out = owned_last[:local]
        owned, begin = [], 0
        for width in widths:
            owned.append(owned_last[local, begin : begin + width])
            begin += width

        mixed = (
            inputs
            + jnp.dot(attended, out_full, preferred_element_type=jnp.float32)
            + jnp.dot(hidden, down_full, preferred_element_type=jnp.float32)
            + attn_bias
            + mlp_bias
        ).astype(jnp.bfloat16)
        normed_grad = attn_in_grad * attn_scale + mlp_in_grad * mlp_scale
        token_grad = (
            inverse
            * (
                normed_grad
                - jnp.mean(normed_grad, axis=1, keepdims=True)
                - normed * jnp.mean(normed_grad * normed, axis=1, keepdims=True)
            )
            + out_grad
        )
        return (
            mixed, token_grad,
            owned_qkv.astype(jnp.float32), owned[0],
            owned_out, owned[1],
            owned_up.astype(jnp.float32), owned[2],
            owned_down.astype(jnp.float32), owned[1],
            owned[3], owned[4], owned[5], owned[6],
        )

    return per_device


def solution(mesh):
    rows, flat = P("dp", None), P("dp")
    return jax.shard_map(
        make(mesh.shape["dp"]),
        mesh=mesh,
        in_specs=(rows, rows, rows, flat) + (rows, flat) * 4 + (flat,) * 4,
        out_specs=(rows, rows) + (rows, flat) * 4 + (flat,) * 4,
        check_vma=False,
    )
```
